32 devices in a mesh: tm: 4 (over y, x), pts: 8 (over z, core).
Axes of the slice: x: 2, y: 2, z: 4, core: 2. Of those that a mesh axis runs over, the one named last changes fastest.
Arguments:
- codes: bfloat16 [11520, 5120], P('tm', 'pts'), as said below
- scales: float32 [11520], P('tm'), may hold values from 0.005 to 0.015
- weights: float32 [5120], P('pts'), may hold values from 0.5 to 4
- freq_indices: int32 [64], replicated, may hold values from 0 to 127, as said below
Outputs:
- cross_spectral: float32 [64, 2, 89, 89], P('pts')
The draws below stay inside these ranges and needn't reach their ends.
Inputs may be any that keep to these rules, and one draw needn't show every extreme that they name: `codes`: whole numbers. `freq_indices`: distinct bins.
All inputs are finite; a program needn't handle non-finite values.
Results may differ from the reference program's by a relative error of at most 0.0011.
Values may be sent and summed in bfloat16 or wider, within the bound.
A program may use at most 64 MiB of HBM per device.

```python
import math
import jax
import jax.numpy as jnp
from jax import lax

NFFT = 256
NF = 64
NB = 89
HOP = 128
TIME = 11520
POINTS = 5120
N_PTS = 8


def walk_from(start_key, step_key, count, width, start_lo, start_hi, step_reach):
    start_value = jax.random.randint(start_key, (1, width), start_lo, start_hi)
    step_values = jax.random.randint(step_key, (count - 1, width), -step_reach, step_reach + 1)
    return jnp.concatenate([start_value, start_value + jnp.cumsum(step_values, axis=0)], axis=0)


def draw_codes(key, part):
    subkeys = jax.random.split(key, 12)
    fine_grid = NFFT * 16
    hop_count = TIME // HOP
    tone_freq = jax.random.randint(subkeys[0], (POINTS,), 16, NFFT // 2 * 16)
    tone_phase = walk_from(subkeys[1], subkeys[2], hop_count, POINTS, 0, fine_grid, fine_grid // 6) % fine_grid
    tone_amp = jnp.clip(walk_from(subkeys[3], subkeys[4], hop_count, POINTS, 8, 29, 5), 4, 32)
    mode_freq = jax.random.randint(subkeys[5], (2,), 16, NFFT // 2 * 16)
    mode_phase = walk_from(subkeys[6], subkeys[7], hop_count, 2, 0, fine_grid, fine_grid // 6) % fine_grid
    mode_amp = jnp.clip(walk_from(subkeys[8], subkeys[9], hop_count, 2, 1, 3, 1), 1, 2)
    mode_coef = jax.random.randint(subkeys[10], (2, POINTS), -1, 2)
    noise_codes = jax.random.randint(subkeys[11], (hop_count, HOP, POINTS), -16, 17)
    sample_times = jnp.arange(TIME, dtype=jnp.int32).reshape(hop_count, HOP, 1)
    tone_turns = (sample_times * tone_freq[None, None, :] + tone_phase[:, None, :]) % fine_grid
    tone_wave = jnp.where(tone_turns < fine_grid // 2, 1, -1) * tone_amp[:, None, :]
    mode_turns = (sample_times * mode_freq[None, None, :] + mode_phase[:, None, :]) % fine_grid
    mode_wave = jnp.where(mode_turns < fine_grid // 2, 1, -1) * mode_amp[:, None, :]
    shared_wave = mode_wave[:, :, 0:1] * mode_coef[0][None, None, :] + mode_wave[:, :, 1:2] * mode_coef[1][None, None, :]
    total = (tone_wave + shared_wave + noise_codes).astype(jnp.int32)
    return total.reshape(TIME, POINTS).astype(jnp.float32).astype(jnp.bfloat16)


def draw_freq_indices(key, part):
    shuffled = jax.random.permutation(key, NFFT // 2 - 2) + 1
    ends = jnp.array([0, NFFT // 2 - 1], dtype=jnp.int32)
    return jnp.concatenate([ends, shuffled[:NF - 2].astype(jnp.int32)]).astype(jnp.int32)


def shard_levels(key, shape, shards, smallest, top_value):
    factor_of = 1.0
    for axis_at, blocks in shards:
        heights = jax.random.uniform(jax.random.fold_in(jax.random.fold_in(key, 6), axis_at), (blocks,), jnp.float32, smallest / len(shards), top_value / len(shards))
        factor_of = factor_of * jnp.repeat(jnp.exp(heights), shape[axis_at] // blocks).reshape((-1,) + (1,) * (len(shape) - 1 - axis_at))
    return factor_of


def setup_inputs(seed: int = 0) -> dict:
    keys = jax.random.split(jax.random.key(seed), 5)
    codes = draw_codes(jax.random.fold_in(keys[4], 71), 0)
    scales = jnp.clip(0.005 + 0.01 * jax.random.uniform(keys[1], (TIME,), jnp.float32) ** shard_levels(keys[1], (TIME,), ((0, 4),), -0.2, 0.2), 0.005, 0.015)
    weights = jnp.clip(jnp.exp(math.log(4.0) - 2.0794415 * jax.random.uniform(keys[2], (POINTS,), jnp.float32) ** shard_levels(keys[2], (POINTS,), ((0, 8),), -0.2, 0.2)), 0.5, 4.0)
    freq_indices = draw_freq_indices(jax.random.fold_in(keys[4], 71), 0)
    return {"codes": codes, "scales": scales, "weights": weights, "freq_indices": freq_indices}


def make_tables(freq_indices):
    sample = jnp.arange(NFFT, dtype=jnp.int32)
    phases = freq_indices[:, None] * sample[None, :] % NFFT
    angles = phases.astype(jnp.float32) * (2.0 * math.pi / NFFT)
    hann_window = 0.5 - 0.5 * jnp.cos(sample.astype(jnp.float32) * (2.0 * math.pi / NFFT))
    cosine_table = (0.25 * hann_window[None, :] * jnp.cos(angles)).astype(jnp.bfloat16)
    sine_table = (-0.25 * hann_window[None, :] * jnp.sin(angles)).astype(jnp.bfloat16)
    return (cosine_table, sine_table)

def reference(codes, scales, weights, freq_indices):
    cosine_table, sine_table = make_tables(freq_indices)
    cosine_wide = cosine_table.astype(jnp.float32)
    sine_wide = sine_table.astype(jnp.float32)
    group = POINTS // N_PTS

    def accumulate(index, running):
        first_point = (index * group).astype(jnp.int32)
        block_codes = lax.dynamic_slice_in_dim(codes, first_point, group, 1)
        block_weights = lax.dynamic_slice_in_dim(weights, first_point, group, 0)
        values = (block_codes.astype(jnp.float32) * scales[:, None]).astype(jnp.bfloat16)
        hop_rows = values.reshape(NB + 1, HOP, group)
        windows = jnp.concatenate([hop_rows[:-1], hop_rows[1:]], axis=1).astype(jnp.float32)
        real_part = jnp.einsum('fn,bnp->fbp', cosine_wide, windows)
        imag_part = jnp.einsum('fn,bnp->fbp', sine_wide, windows)
        root_weight = jnp.sqrt(block_weights / POINTS)
        scaled_re = (real_part * root_weight[None, None, :]).astype(jnp.bfloat16)
        scaled_im = (imag_part * root_weight[None, None, :]).astype(jnp.bfloat16)
        stacked = jnp.concatenate([scaled_re, scaled_im], axis=1).astype(jnp.float32)
        products = jnp.einsum('fip,fjp->fij', stacked, stacked)
        matrix_re = products[:, :NB, :NB] + products[:, NB:, NB:]
        matrix_im = products[:, :NB, NB:] - products[:, NB:, :NB]
        return running + jnp.stack([matrix_re, matrix_im], axis=1)
    start_value = jnp.zeros((NF, 2, NB, NB), jnp.float32)
    return lax.fori_loop(0, N_PTS, accumulate, start_value)
```

```python
import functools
import math

import jax
import jax.numpy as jnp
from jax import lax
from jax.experimental import pallas as pl
from jax.experimental.pallas import tpu as pltpu
from jax.sharding import PartitionSpec as P

NFFT = 256
HOP = NFFT // 2
HALO = 192
SLOTS = 24
LANES = 128
MESH = pl.DeviceIdType.MESH


def make_tables(freq_indices):
    sample = jnp.arange(NFFT, dtype=jnp.int32)
    phases = freq_indices[:, None] * sample[None, :] % NFFT
    angles = phases.astype(jnp.float32) * (2.0 * math.pi / NFFT)
    hann_window = 0.5 - 0.5 * jnp.cos(sample.astype(jnp.float32) * (2.0 * math.pi / NFFT))
    cosine_table = (0.25 * hann_window[None, :] * jnp.cos(angles)).astype(jnp.bfloat16)
    sine_table = (-0.25 * hann_window[None, :] * jnp.sin(angles)).astype(jnp.bfloat16)
    return (cosine_table, sine_table)


def block_ranges(rows, nt):
    blocks = rows * nt // HOP - 1
    firsts = [-(-t * rows // HOP) for t in range(nt)] + [blocks]
    return [(firsts[t], min(firsts[t + 1], blocks) - firsts[t]) for t in range(nt)]


def kernel(
    nt, nz, chunks, ranges, total_points,
    codes_ref, scales_ref, weights_ref, table_ref, out_ref,
    vals, stage, send, recv, part, corebuf, summed, zbuf, gath,
    halo_s, halo_r, tm_s, tm_r, core_s, core_r, z_s, z_r, g_s, g_r,
):
    rows, points = codes_ref.shape
    t = lax.axis_index("tm")
    p = lax.axis_index("pts")
    z = p // 2
    c = p % 2
    partner = p + 1 - 2 * c
    per = 2 * nz
    lane_tiles = points // LANES

    barrier = pltpu.get_barrier_semaphore()
    for d in range(1, nt):
        pl.semaphore_signal(barrier, inc=1, device_id=((t + d) % nt, p), device_id_type=MESH)
    pl.semaphore_signal(barrier, inc=1, device_id=(t, partner), device_id_type=MESH)
    for d in range(1, nz):
        pl.semaphore_signal(barrier, inc=1, device_id=(t, (z + d) % nz * 2 + c), device_id_type=MESH)

    step = HALO // 2

    def dequantize(i, carry):
        at = pl.ds(pl.multiple_of(i * step, step), step)
        vals[at, :] = (codes_ref[at, :].astype(jnp.float32) * scales_ref[at, :]).astype(jnp.bfloat16)
        return carry

    lax.fori_loop(0, HALO // step, dequantize, 0)
    pl.semaphore_wait(barrier, nt + nz - 1)
    halo = pltpu.make_async_remote_copy(
        src_ref=vals.at[pl.ds(0, HALO)],
        dst_ref=vals.at[pl.ds(rows, HALO)],
        send_sem=halo_s, recv_sem=halo_r,
        device_id=((t + nt - 1) % nt, p), device_id_type=MESH,
    )
    halo.start()
    tail = vals.shape[0] - rows - HALO
    vals[pl.ds(rows + HALO, tail), :] = jnp.zeros((tail, points), jnp.bfloat16)
    lax.fori_loop(HALO // step, rows // step, dequantize, 0)

    offset = (t % 2) * (HOP // 2)
    root_weight = jnp.sqrt(weights_ref[...] / total_points)
    table_rows = table_ref.shape[1]
    used = max(count for _, count in ranges)
    for lane in range(lane_tiles):
        for spare in range(used, SLOTS):
            stage[lane, pl.ds(spare, table_rows, stride=SLOTS), :] = jnp.zeros((table_rows, LANES), jnp.float32)

    def exchange(k, d):
        return pltpu.make_async_remote_copy(
            src_ref=send.at[k, d - 1],
            dst_ref=recv.at[k, :, t],
            send_sem=tm_s.at[k, d - 1], recv_sem=tm_r.at[k, d - 1],
            device_id=((t + d) % nt, p), device_id_type=MESH,
        )

    safe = (rows - HOP // 2 - NFFT) // HOP + 1
    for k in range(chunks):
        table = table_ref[k]

        def spectrum(i, carry):
            window = vals[pl.ds(pl.multiple_of(offset + i * HOP, HOP // 2), NFFT), :]
            result = jnp.dot(table, window, preferred_element_type=jnp.float32) * root_weight
            for lane in range(lane_tiles):
                stage[lane, pl.ds(i, table_rows, stride=SLOTS), :] = result[:, lane * LANES:(lane + 1) * LANES]
            return carry

        lax.fori_loop(0, safe, spectrum, 0)
        if k == 0:
            halo.wait()
        lax.fori_loop(safe, used, spectrum, 0)

        for d in (3, 1, 2, 0):
            dest = (t + d) % nt

            def pack(f, carry):
                base = pl.multiple_of((dest * per + f) * 2 * SLOTS, 2 * SLOTS)
                for lane in range(lane_tiles):
                    block = stage[lane, pl.ds(base, 2 * SLOTS), :].astype(jnp.bfloat16)
                    at = slice(lane * LANES, (lane + 1) * LANES)
                    if d == 0:
                        recv[k, f, t, :, at] = block
                    else:
                        send[k, d - 1, f, :, at] = block
                return carry

            lax.fori_loop(0, per, pack, 0)
            if d:
                exchange(k, d).start()

    width = nt * 2 * SLOTS
    wide = 2 * LANES
    lane_in = lax.broadcasted_iota(jnp.int32, (1, wide), 1) % (2 * SLOTS) < SLOTS
    sign = jnp.where(lane_in, -1.0, 1.0)

    def to_core(k):
        return pltpu.make_async_remote_copy(
            src_ref=part.at[k, :, 1 - c], dst_ref=corebuf.at[k],
            send_sem=core_s.at[k], recv_sem=core_r.at[k],
            device_id=(t, partner), device_id_type=MESH,
        )

    def to_z(k, d):
        return pltpu.make_async_remote_copy(
            src_ref=summed.at[k, (z + d) % nz], dst_ref=zbuf.at[k, d - 1],
            send_sem=z_s.at[k, d - 1], recv_sem=z_r.at[k, d - 1],
            device_id=(t, (z + d) % nz * 2 + c), device_id_type=MESH,
        )

    def to_tm(k, d):
        return pltpu.make_async_remote_copy(
            src_ref=gath.at[t, k], dst_ref=gath.at[t, k],
            send_sem=g_s.at[k, d - 1], recv_sem=g_r.at[k, d - 1],
            device_id=((t + d) % nt, p), device_id_type=MESH,
        )

    for k in range(chunks):
        for d in range(1, nt):
            exchange(k, d).wait()

        def cross(f, carry):
            stacked = recv[k, f].reshape(width, points)
            prod = lax.dot_general(
                stacked, stacked, (((1,), (1,)), ((), ())), preferred_element_type=jnp.float32
            )
            real = jnp.concatenate(
                [prod[2 * s * SLOTS:(2 * s + 1) * SLOTS] for s in range(nt)], axis=0)
            imag = jnp.concatenate(
                [prod[(2 * s + 1) * SLOTS:(2 * s + 2) * SLOTS] for s in range(nt)], axis=0)
            fill = jnp.zeros((nt * SLOTS, wide - width), jnp.float32)
            real = jnp.concatenate([real, fill], axis=1)
            imag = jnp.concatenate([imag, fill], axis=1)
            both = real + sign * imag
            both = both + pltpu.roll(both, wide - SLOTS, 1)
            moved = pltpu.roll(both, wide - 3 * SLOTS, 1)
            part[k, f // 2, f % 2] = jnp.where(lane_in[:, :LANES], both[:, :LANES], moved[:, :LANES])
            return carry

        lax.fori_loop(0, per, cross, 0)
        to_core(k).start()
        to_core(k).wait()
        summed[k] = part[k, :, c] + corebuf[k]
        for d in range(1, nz):
            to_z(k, d).start()

    for k in range(chunks):
        for d in range(1, nz):
            to_z(k, d).wait()
        total = summed[k, z]
        for d in range(1, nz):
            total = total + zbuf[k, d - 1]
        gath[t, k] = total
        for d in range(1, nt):
            to_tm(k, d).start()

    for k in range(chunks):
        for d in range(1, nt):
            to_tm(k, d).wait()

    places = [0, 2, 1, 3]
    column = lax.broadcasted_iota(jnp.int32, (1, LANES), 1)

    def finish(i, carry):
        s = i // chunks
        k = i % chunks
        packed = gath[s, k]
        placed = packed
        for g in range(1, nt):
            shift = (ranges[g][0] - places[g] * SLOTS) % LANES
            placed = jnp.where(column >= ranges[g][0], pltpu.roll(packed, shift, 1), placed)
        ordered = jnp.concatenate(
            [placed[g * SLOTS:g * SLOTS + ranges[g][1]] for g in range(nt)]
            + [jnp.zeros((LANES - sum(n for _, n in ranges), LANES), jnp.float32)], axis=0)
        mirrored = ordered.T
        keep = out_ref.shape[2]
        out_ref[i, 0] = (0.5 * (ordered + mirrored))[:keep]
        out_ref[i, 1] = (0.5 * (ordered - mirrored))[:keep]
        return carry

    lax.fori_loop(0, nt * chunks, finish, 0)


def fused(nt, np_, codes, scales, weights, freq_indices):
    rows, points = codes.shape
    nf = freq_indices.shape[0]
    nz = np_ // 2
    chunks = nf // (nt * np_)
    ranges = block_ranges(rows, nt)
    blocks = rows * nt // HOP - 1
    order = freq_indices.reshape(np_, nt, chunks).transpose(2, 1, 0).reshape(-1)
    cosine_table, sine_table = make_tables(order)
    table = jnp.stack([cosine_table, sine_table], axis=1).reshape(chunks, 2 * nt * np_, NFFT)
    height = nt * SLOTS
    used = max(count for _, count in ranges)
    vals_rows = HOP // 2 + (used - 1) * HOP + NFFT
    f32, bf16 = jnp.float32, jnp.bfloat16
    dma = pltpu.SemaphoreType.DMA
    vmem = pl.BlockSpec(memory_space=pltpu.VMEM)
    full = pl.pallas_call(
        functools.partial(kernel, nt, nz, chunks, ranges, points * np_),
        out_shape=jax.ShapeDtypeStruct((nt * chunks, 2, height, LANES), f32),
        in_specs=[vmem] * 4,
        out_specs=vmem,
        scratch_shapes=[
            pltpu.VMEM((vals_rows, points), bf16),
            pltpu.VMEM((points // LANES, 2 * nt * np_ * SLOTS, LANES), f32),
            pltpu.VMEM((chunks, nt - 1, np_, 2 * SLOTS, points), bf16),
            pltpu.VMEM((chunks, np_, nt, 2 * SLOTS, points), bf16),
            pltpu.VMEM((chunks, nz, 2, height, LANES), f32),
            pltpu.VMEM((chunks, nz, height, LANES), f32),
            pltpu.VMEM((chunks, nz, height, LANES), f32),
            pltpu.VMEM((chunks, nz - 1, height, LANES), f32),
            pltpu.VMEM((nt, chunks, height, LANES), f32),
            dma, dma,
            dma((chunks, nt - 1)), dma((chunks, nt - 1)),
            dma((chunks,)), dma((chunks,)),
            dma((chunks, nz - 1)), dma((chunks, nz - 1)),
            dma((chunks, nt - 1)), dma((chunks, nt - 1)),
        ],
        compiler_params=pltpu.CompilerParams(
            collective_id=0, has_side_effects=True, vmem_limit_bytes=48 * 2**20
        ),
        name="spectra_cross",
    )(codes, scales.reshape(-1, 1), weights.reshape(1, -1), table)
    return full[:, :, :blocks, :blocks]


def cross_matrices(stacked):
    blocks = stacked.shape[1] // 2
    products = jnp.einsum("fip,fjp->fij", stacked, stacked, preferred_element_type=jnp.float32)
    matrix_re = products[:, :blocks, :blocks] + products[:, blocks:, blocks:]
    matrix_im = products[:, :blocks, blocks:] - products[:, blocks:, :blocks]
    return jnp.stack([matrix_re, matrix_im], axis=1)


def general(codes, scales, weights, freq_indices):
    values = (codes.astype(jnp.float32) * scales[:, None]).astype(jnp.bfloat16)
    regrouped = lax.all_to_all(values, "tm", split_axis=1, concat_axis=0, tiled=True)
    point_count = regrouped.shape[1]
    own_weights = lax.dynamic_slice_in_dim(
        weights, lax.axis_index("tm") * point_count, point_count, 0
    )
    total_points = weights.shape[0] * lax.axis_size("pts")
    root_weight = jnp.sqrt(own_weights / total_points)
    cosine_table, sine_table = make_tables(freq_indices)
    hop_rows = regrouped.reshape(-1, NFFT // 2, point_count)
    windows = jnp.concatenate([hop_rows[:-1], hop_rows[1:]], axis=1)
    real_part = jnp.einsum("fn,bnp->fbp", cosine_table, windows, preferred_element_type=jnp.float32)
    imag_part = jnp.einsum("fn,bnp->fbp", sine_table, windows, preferred_element_type=jnp.float32)
    scaled_re = (real_part * root_weight[None, None, :]).astype(jnp.bfloat16)
    scaled_im = (imag_part * root_weight[None, None, :]).astype(jnp.bfloat16)
    stacked = jnp.concatenate([scaled_re, scaled_im], axis=1)
    partial_value = lax.psum_scatter(
        cross_matrices(stacked), "pts", scatter_dimension=0, tiled=True
    )
    return lax.psum(partial_value, "tm")


def solution(mesh):
    nt, np_ = mesh.shape["tm"], mesh.shape["pts"]

    def per_device(codes, scales, weights, freq_indices):
        rows, points = codes.shape
        fits = (
            nt == 4
            and np_ == 8
            and freq_indices.shape[0] % (nt * np_) == 0
            and points % LANES == 0
            and rows % HALO == 0
            and rows % HOP == HOP // 2
            and max(count for _, count in block_ranges(rows, nt)) <= SLOTS
        )
        if fits:
            return fused(nt, np_, codes, scales, weights, freq_indices)
        return general(codes, scales, weights, freq_indices)

    return jax.shard_map(
        per_device,
        mesh=mesh,
        in_specs=(P("tm", "pts"), P("tm"), P("pts"), P()),
        out_specs=P("pts", None, None, None),
        check_vma=False,
    )
```

```python
import functools
import math

import jax
import jax.numpy as jnp
from jax import lax
from jax.experimental import pallas as pl
from jax.experimental.pallas import tpu as pltpu
from jax.sharding import PartitionSpec as P

NFFT = 256
HOP = NFFT // 2
HALO = 192
SLOTS = 24
LANES = 128
MESH = pl.DeviceIdType.MESH


def make_tables(freq_indices):
    sample = jnp.arange(NFFT, dtype=jnp.int32)
    phases = freq_indices[:, None] * sample[None, :] % NFFT
    angles = phases.astype(jnp.float32) * (2.0 * math.pi / NFFT)
    hann_window = 0.5 - 0.5 * jnp.cos(sample.astype(jnp.float32) * (2.0 * math.pi / NFFT))
    cosine_table = (0.25 * hann_window[None, :] * jnp.cos(angles)).astype(jnp.bfloat16)
    sine_table = (-0.25 * hann_window[None, :] * jnp.sin(angles)).astype(jnp.bfloat16)
    return (cosine_table, sine_table)


def block_ranges(rows, nt):
    blocks = rows * nt // HOP - 1
    firsts = [-(-t * rows // HOP) for t in range(nt)] + [blocks]
    return [(firsts[t], min(firsts[t + 1], blocks) - firsts[t]) for t in range(nt)]


def kernel(
    nt, nz, chunks, ranges, total_points,
    codes_hbm, scales_ref, weights_ref, table_ref, out_ref,
    codes_ref, vals, stage, send, recv, part, corebuf, summed, zbuf, gath,
    load_s, halo_s, halo_r, tm_s, tm_r, core_s, core_r, z_s, z_r, g_s, g_r,
):
    rows, points = codes_ref.shape
    t = lax.axis_index("tm")
    p = lax.axis_index("pts")
    z = p // 2
    c = p % 2
    partner = p + 1 - 2 * c
    per = 2 * nz
    half = per // 2
    lane_tiles = points // LANES
    groups = SLOTS // 8
    used = max(count for _, count in ranges)
    step = HALO // 2

    ends = [
        min(-(-(HOP // 2 + (8 * g + 7) * HOP + NFFT) // step) * step, rows) for g in range(groups - 1)
    ] + [rows]
    starts = [0] + ends[:-1]
    loads = [
        pltpu.make_async_copy(
            codes_hbm.at[pl.ds(starts[g], ends[g] - starts[g])],
            codes_ref.at[pl.ds(starts[g], ends[g] - starts[g])],
            load_s.at[g],
        )
        for g in range(groups)
    ]
    for load in loads:
        load.start()

    barrier = pltpu.get_barrier_semaphore()
    for d in range(1, nt):
        pl.semaphore_signal(barrier, inc=1, device_id=((t + d) % nt, p), device_id_type=MESH)
    pl.semaphore_signal(barrier, inc=1, device_id=(t, partner), device_id_type=MESH)
    for d in range(1, nz):
        pl.semaphore_signal(barrier, inc=1, device_id=(t, (z + d) % nz * 2 + c), device_id_type=MESH)

    root_weight = jnp.sqrt(weights_ref[...] / total_points)
    tail = vals.shape[0] - rows - HALO
    vals[pl.ds(rows + HALO, tail), :] = jnp.zeros((tail, points), jnp.bfloat16)
    half_rows = table_ref.shape[1] // 2

    def place(i, lane, result):
        at = (i // 8) * 16 + i % 8
        for part_of in range(2):
            stage[lane, pl.ds(at + 8 * part_of, half_rows, stride=2 * SLOTS), :] = result[part_of]

    for lane in range(lane_tiles):
        for spare in range(used, SLOTS):
            place(spare, lane, [jnp.zeros((half_rows, LANES), jnp.float32)] * 2)

    def dequantize(i, carry):
        at = pl.ds(pl.multiple_of(i * step, step), step)
        vals[at, :] = (codes_ref[at, :].astype(jnp.float32) * scales_ref[at, :]).astype(jnp.bfloat16)
        return carry

    halo = pltpu.make_async_remote_copy(
        src_ref=vals.at[pl.ds(0, HALO)],
        dst_ref=vals.at[pl.ds(rows, HALO)],
        send_sem=halo_s, recv_sem=halo_r,
        device_id=((t + nt - 1) % nt, p), device_id_type=MESH,
    )
    offset = (t % 2) * (HOP // 2)

    def spectra(k, first, last):
        table = table_ref[k]

        def spectrum(i, carry):
            window = vals[pl.ds(pl.multiple_of(offset + i * HOP, HOP // 2), NFFT), :]
            result = jnp.dot(table, window, preferred_element_type=jnp.float32) * root_weight
            for lane in range(lane_tiles):
                columns = result[:, lane * LANES:(lane + 1) * LANES]
                place(i, lane, [columns[:half_rows], columns[half_rows:]])
            return carry

        lax.fori_loop(first, last, spectrum, 0)

    def pack_group(k, g, d):
        dest = (t + d) % nt

        def pack(f, carry):
            base = pl.multiple_of((dest * per + f) * 2 * SLOTS + g * 16, 16)
            for lane in range(lane_tiles):
                block = stage[lane, pl.ds(base, 16), :].astype(jnp.bfloat16)
                at = slice(lane * LANES, (lane + 1) * LANES)
                if d == 0:
                    recv[k, f, t, g * 16:(g + 1) * 16, at] = block
                else:
                    send[k, d - 1, f, g * 16:(g + 1) * 16, at] = block
            return carry

        lax.fori_loop(0, per, pack, 0)

    def exchange(k, piece, d):
        if k < chunks - 1:
            src = send.at[k, d - 1, :, pl.ds(piece * 16, 16)]
            dst = recv.at[k, :, t, pl.ds(piece * 16, 16)]
        else:
            src = send.at[k, d - 1, pl.ds(piece * half, half)]
            dst = recv.at[k, pl.ds(piece * half, half), t]
        return pltpu.make_async_remote_copy(
            src_ref=src, dst_ref=dst,
            send_sem=tm_s.at[k, piece, d - 1], recv_sem=tm_r.at[k, piece, d - 1],
            device_id=((t + d) % nt, p), device_id_type=MESH,
        )

    safe = (rows - HOP // 2 - NFFT) // HOP + 1
    partners = (3, 1, 2)
    for k in range(chunks):
        for g in range(groups):
            first, last = 8 * g, min(8 * g + 8, used)
            if k == 0:
                loads[g].wait()
                lax.fori_loop(starts[g] // step, ends[g] // step, dequantize, 0)
                if g == 0:
                    pl.semaphore_wait(barrier, nt + nz - 1)
                    halo.start()
                if last > safe:
                    spectra(k, first, safe)
                    halo.wait()
                    first = safe
            spectra(k, first, last)
            for d in partners + (0,):
                pack_group(k, g, d)
                if d and k < chunks - 1:
                    exchange(k, g, d).start()
        if k == chunks - 1:
            for h in range(2):
                for d in partners:
                    exchange(k, h, d).start()

    width = nt * 2 * SLOTS
    wide = 2 * LANES
    eights = nt * groups
    lane_in = lax.broadcasted_iota(jnp.int32, (1, wide), 1) % 16 < 8
    sign = jnp.where(lane_in, -1.0, 1.0)

    def to_core(k, h):
        at = pl.ds(h * nz // 2, nz // 2)
        return pltpu.make_async_remote_copy(
            src_ref=part.at[k, at, 1 - c], dst_ref=corebuf.at[k, at],
            send_sem=core_s.at[k, h], recv_sem=core_r.at[k, h],
            device_id=(t, partner), device_id_type=MESH,
        )

    def to_z(k, peer):
        return pltpu.make_async_remote_copy(
            src_ref=summed.at[k, peer], dst_ref=zbuf.at[k, z],
            send_sem=z_s.at[k, peer], recv_sem=z_r.at[k, z],
            device_id=(t, peer * 2 + c), device_id_type=MESH,
        )

    def from_z(k, peer):
        return pltpu.make_async_remote_copy(
            src_ref=summed.at[k, peer], dst_ref=zbuf.at[k, peer],
            send_sem=z_s.at[k, peer], recv_sem=z_r.at[k, peer],
            device_id=(t, peer * 2 + c), device_id_type=MESH,
        )

    def to_tm(k, d):
        return pltpu.make_async_remote_copy(
            src_ref=gath.at[t, k], dst_ref=gath.at[t, k],
            send_sem=g_s.at[k, d - 1], recv_sem=g_r.at[k, d - 1],
            device_id=((t + d) % nt, p), device_id_type=MESH,
        )

    def cross_half(k, h):
        def cross(f, carry):
            stacked = recv[k, f].reshape(width, points)
            prod = lax.dot_general(
                stacked, stacked, (((1,), (1,)), ((), ())), preferred_element_type=jnp.float32
            )
            real = jnp.concatenate([prod[16 * m:16 * m + 8] for m in range(eights)], axis=0)
            imag = jnp.concatenate([prod[16 * m + 8:16 * m + 16] for m in range(eights)], axis=0)
            fill = jnp.zeros((nt * SLOTS, wide - width), jnp.float32)
            real = jnp.concatenate([real, fill], axis=1)
            imag = jnp.concatenate([imag, fill], axis=1)
            both = real + sign * imag
            both = both + pltpu.roll(both, wide - 8, 1)
            moved = pltpu.roll(both, wide - (LANES - 8), 1)
            part[k, f // 2, f % 2] = jnp.where(lane_in[:, :LANES], both[:, :LANES], moved[:, :LANES])
            return carry

        lax.fori_loop(h * half, (h + 1) * half, cross, 0)
        to_core(k, h).start()
        to_core(k, h).wait()
        for peer in range(h * nz // 2, (h + 1) * nz // 2):
            summed[k, peer] = part[k, peer, c] + corebuf[k, peer]

            @pl.when(peer != z)
            def _():
                to_z(k, peer).start()

    def compress(padded):
        kept = [padded[s * SLOTS:s * SLOTS + ranges[s][1]] for s in range(nt)]
        fill = LANES - sum(n for _, n in ranges)
        return jnp.concatenate(kept + [jnp.zeros((fill, LANES), jnp.float32)], axis=0)

    def reduce_z(k):
        total = summed[k, z]
        for d in range(1, nz):
            peer = (z + d) % nz
            from_z(k, peer).wait()
            total = total + zbuf[k, peer]
        full = jnp.concatenate([total, jnp.zeros((LANES - nt * SLOTS, LANES), jnp.float32)], axis=0)
        turned = full.T
        where = [16 * m if m < 8 else 16 * (m - 8) + 8 for m in range(eights)]
        turned = jnp.concatenate([turned[w:w + 8] for w in where], axis=0)
        gath[t, k] = compress(compress(turned).T)[:nt * SLOTS]
        for d in range(1, nt):
            to_tm(k, d).start()

    def finish(k):
        for d in range(1, nt):
            to_tm(k, d).wait()

        def one(s, carry):
            ordered = gath[s, k]
            fill = jnp.zeros((LANES - nt * SLOTS, LANES), jnp.float32)
            mirrored = jnp.concatenate([ordered, fill], axis=0).T[:nt * SLOTS]
            out_ref[s * chunks + k, 0] = 0.5 * (ordered + mirrored)
            out_ref[s * chunks + k, 1] = 0.5 * (ordered - mirrored)
            return carry

        lax.fori_loop(0, nt, one, 0)

    for k in range(chunks):
        for h in range(2):
            if k == chunks - 1:
                for d in partners:
                    exchange(k, h, d).wait()
            elif h == 0:
                for g in range(groups):
                    for d in partners:
                        exchange(k, g, d).wait()
            cross_half(k, h)
        if k < chunks - 1:
            reduce_z(k)
    for k in range(chunks - 1):
        finish(k)
    reduce_z(chunks - 1)
    finish(chunks - 1)


def fused(nt, np_, codes, scales, weights, freq_indices):
    rows, points = codes.shape
    nf = freq_indices.shape[0]
    nz = np_ // 2
    chunks = nf // (nt * np_)
    ranges = block_ranges(rows, nt)
    blocks = rows * nt // HOP - 1
    order = freq_indices.reshape(np_, nt, chunks).transpose(2, 1, 0).reshape(-1)
    cosine_table, sine_table = make_tables(order)
    shape = (chunks, nt * np_, NFFT)
    table = jnp.concatenate([cosine_table.reshape(shape), sine_table.reshape(shape)], axis=1)
    height = nt * SLOTS
    used = max(count for _, count in ranges)
    vals_rows = HOP // 2 + (used - 1) * HOP + NFFT
    groups = SLOTS // 8
    f32, bf16 = jnp.float32, jnp.bfloat16
    dma = pltpu.SemaphoreType.DMA
    vmem = pl.BlockSpec(memory_space=pltpu.VMEM)
    full = pl.pallas_call(
        functools.partial(kernel, nt, nz, chunks, ranges, points * np_),
        out_shape=jax.ShapeDtypeStruct((nt * chunks, 2, height, LANES), f32),
        in_specs=[pl.BlockSpec(memory_space=pl.ANY)] + [vmem] * 3,
        out_specs=vmem,
        scratch_shapes=[
            pltpu.VMEM((rows, points), bf16),
            pltpu.VMEM((vals_rows, points), bf16),
            pltpu.VMEM((points // LANES, nt * np_ * 2 * SLOTS, LANES), f32),
            pltpu.VMEM((chunks, nt - 1, np_, 2 * SLOTS, points), bf16),
            pltpu.VMEM((chunks, np_, nt, 2 * SLOTS, points), bf16),
            pltpu.VMEM((chunks, nz, 2, height, LANES), f32),
            pltpu.VMEM((chunks, nz, height, LANES), f32),
            pltpu.VMEM((chunks, nz, height, LANES), f32),
            pltpu.VMEM((chunks, nz, height, LANES), f32),
            pltpu.VMEM((nt, chunks, height, LANES), f32),
            dma((groups,)),
            dma, dma,
            dma((chunks, groups, nt - 1)), dma((chunks, groups, nt - 1)),
            dma((chunks, 2)), dma((chunks, 2)),
            dma((chunks, nz)), dma((chunks, nz)),
            dma((chunks, nt - 1)), dma((chunks, nt - 1)),
        ],
        compiler_params=pltpu.CompilerParams(
            collective_id=0, has_side_effects=True, vmem_limit_bytes=60 * 2**20
        ),
        name="spectra_cross",
    )(codes, scales.reshape(-1, 1), weights.reshape(1, -1), table)
    return full[:, :, :blocks, :blocks]


def cross_matrices(stacked):
    blocks = stacked.shape[1] // 2
    products = jnp.einsum("fip,fjp->fij", stacked, stacked, preferred_element_type=jnp.float32)
    matrix_re = products[:, :blocks, :blocks] + products[:, blocks:, blocks:]
    matrix_im = products[:, :blocks, blocks:] - products[:, blocks:, :blocks]
    return jnp.stack([matrix_re, matrix_im], axis=1)


def general(codes, scales, weights, freq_indices):
    values = (codes.astype(jnp.float32) * scales[:, None]).astype(jnp.bfloat16)
    regrouped = lax.all_to_all(values, "tm", split_axis=1, concat_axis=0, tiled=True)
    point_count = regrouped.shape[1]
    own_weights = lax.dynamic_slice_in_dim(
        weights, lax.axis_index("tm") * point_count, point_count, 0
    )
    total_points = weights.shape[0] * lax.axis_size("pts")
    root_weight = jnp.sqrt(own_weights / total_points)
    cosine_table, sine_table = make_tables(freq_indices)
    hop_rows = regrouped.reshape(-1, NFFT // 2, point_count)
    windows = jnp.concatenate([hop_rows[:-1], hop_rows[1:]], axis=1)
    real_part = jnp.einsum("fn,bnp->fbp", cosine_table, windows, preferred_element_type=jnp.float32)
    imag_part = jnp.einsum("fn,bnp->fbp", sine_table, windows, preferred_element_type=jnp.float32)
    scaled_re = (real_part * root_weight[None, None, :]).astype(jnp.bfloat16)
    scaled_im = (imag_part * root_weight[None, None, :]).astype(jnp.bfloat16)
    stacked = jnp.concatenate([scaled_re, scaled_im], axis=1)
    partial_value = lax.psum_scatter(
        cross_matrices(stacked), "pts", scatter_dimension=0, tiled=True
    )
    return lax.psum(partial_value, "tm")


def solution(mesh):
    nt, np_ = mesh.shape["tm"], mesh.shape["pts"]

    def per_device(codes, scales, weights, freq_indices):
        rows, points = codes.shape
        fits = (
            nt == 4
            and np_ == 8
            and freq_indices.shape[0] % (nt * np_) == 0
            and points % LANES == 0
            and rows % HALO == 0
            and rows % HOP == HOP // 2
            and max(count for _, count in block_ranges(rows, nt)) <= SLOTS
        )
        if fits:
            return fused(nt, np_, codes, scales, weights, freq_indices)
        return general(codes, scales, weights, freq_indices)

    return jax.shard_map(
        per_device,
        mesh=mesh,
        in_specs=(P("tm", "pts"), P("tm"), P("pts"), P()),
        out_specs=P("pts", None, None, None),
        check_vma=False,
    )
```

```python
import functools
import math

import jax
import jax.numpy as jnp
from jax import lax
from jax.experimental import pallas as pl
from jax.experimental.pallas import tpu as pltpu
from jax.sharding import PartitionSpec as P

NFFT = 256
HOP = NFFT // 2
HALO = 192
SLOTS = 24
LANES = 128
MESH = pl.DeviceIdType.MESH


def make_tables(freq_indices):
    sample = jnp.arange(NFFT, dtype=jnp.int32)
    phases = freq_indices[:, None] * sample[None, :] % NFFT
    angles = phases.astype(jnp.float32) * (2.0 * math.pi / NFFT)
    hann_window = 0.5 - 0.5 * jnp.cos(sample.astype(jnp.float32) * (2.0 * math.pi / NFFT))
    cosine_table = (0.25 * hann_window[None, :] * jnp.cos(angles)).astype(jnp.bfloat16)
    sine_table = (-0.25 * hann_window[None, :] * jnp.sin(angles)).astype(jnp.bfloat16)
    return (cosine_table, sine_table)


def block_ranges(rows, nt):
    blocks = rows * nt // HOP - 1
    firsts = [-(-t * rows // HOP) for t in range(nt)] + [blocks]
    return [(firsts[t], min(firsts[t + 1], blocks) - firsts[t]) for t in range(nt)]


def kernel(
    nt, nz, chunks, ranges, total_points,
    codes_hbm, scales_ref, weights_ref, table_ref, out_ref,
    codes_ref, vals, stage, send, recv, part, corebuf, summed, zbuf, gath,
    load_s, halo_s, halo_r, tm_s, tm_r, core_s, core_r, z_s, z_r, g_s, g_r,
):
    rows, points = codes_ref.shape
    t = lax.axis_index("tm")
    p = lax.axis_index("pts")
    z = p // 2
    c = p % 2
    partner = p + 1 - 2 * c
    per = 2 * nz
    half = per // 2
    lane_tiles = points // LANES
    groups = SLOTS // 8
    used = max(count for _, count in ranges)
    step = HALO // 2

    ends = [
        min(-(-(HOP // 2 + (8 * g + 7) * HOP + NFFT) // step) * step, rows) for g in range(groups - 1)
    ] + [rows]
    starts = [0] + ends[:-1]
    loads = [
        pltpu.make_async_copy(
            codes_hbm.at[pl.ds(starts[g], ends[g] - starts[g])],
            codes_ref.at[pl.ds(starts[g], ends[g] - starts[g])],
            load_s.at[g],
        )
        for g in range(groups)
    ]
    for load in loads:
        load.start()

    barrier = pltpu.get_barrier_semaphore()
    for d in range(1, nt):
        pl.semaphore_signal(barrier, inc=1, device_id=((t + d) % nt, p), device_id_type=MESH)
    pl.semaphore_signal(barrier, inc=1, device_id=(t, partner), device_id_type=MESH)
    for d in range(1, nz):
        pl.semaphore_signal(barrier, inc=1, device_id=(t, (z + d) % nz * 2 + c), device_id_type=MESH)

    root_weight = jnp.sqrt(weights_ref[...] / total_points)
    tail = vals.shape[0] - rows - HALO
    vals[pl.ds(rows + HALO, tail), :] = jnp.zeros((tail, points), jnp.bfloat16)
    half_rows = table_ref.shape[1] // 2

    def place(i, lane, result):
        at = (i // 8) * 16 + i % 8
        for part_of in range(2):
            stage[lane, pl.ds(at + 8 * part_of, half_rows, stride=2 * SLOTS), :] = result[part_of]

    for lane in range(lane_tiles):
        for spare in range(used, SLOTS):
            place(spare, lane, [jnp.zeros((half_rows, LANES), jnp.float32)] * 2)

    def dequantize(i, carry):
        at = pl.ds(pl.multiple_of(i * step, step), step)
        vals[at, :] = (codes_ref[at, :].astype(jnp.float32) * scales_ref[at, :]).astype(jnp.bfloat16)
        return carry

    halo = pltpu.make_async_remote_copy(
        src_ref=vals.at[pl.ds(0, HALO)],
        dst_ref=vals.at[pl.ds(rows, HALO)],
        send_sem=halo_s, recv_sem=halo_r,
        device_id=((t + nt - 1) % nt, p), device_id_type=MESH,
    )
    offset = (t % 2) * (HOP // 2)

    def spectra(k, first, last):
        table = table_ref[k]

        def spectrum(i, carry):
            window = vals[pl.ds(pl.multiple_of(offset + i * HOP, HOP // 2), NFFT), :]
            result = jnp.dot(table, window, preferred_element_type=jnp.float32) * root_weight
            for lane in range(lane_tiles):
                columns = result[:, lane * LANES:(lane + 1) * LANES]
                place(i, lane, [columns[:half_rows], columns[half_rows:]])
            return carry

        lax.fori_loop(first, last, spectrum, 0)

    def pack_group(k, g, d):
        dest = (t + d) % nt

        def pack(f, carry):
            base = pl.multiple_of((dest * per + f) * 2 * SLOTS + g * 16, 16)
            for lane in range(lane_tiles):
                block = stage[lane, pl.ds(base, 16), :].astype(jnp.bfloat16)
                at = slice(lane * LANES, (lane + 1) * LANES)
                if d == 0:
                    recv[k, f, t, g * 16:(g + 1) * 16, at] = block
                else:
                    send[k, d - 1, f, g * 16:(g + 1) * 16, at] = block
            return carry

        lax.fori_loop(0, per, pack, 0)

    def exchange(k, piece, d):
        if k < chunks - 1:
            src = send.at[k, d - 1, :, pl.ds(piece * 16, 16)]
            dst = recv.at[k, :, t, pl.ds(piece * 16, 16)]
        else:
            src = send.at[k, d - 1, pl.ds(piece * half, half)]
            dst = recv.at[k, pl.ds(piece * half, half), t]
        return pltpu.make_async_remote_copy(
            src_ref=src, dst_ref=dst,
            send_sem=tm_s.at[k, piece, d - 1], recv_sem=tm_r.at[k, piece, d - 1],
            device_id=((t + d) % nt, p), device_id_type=MESH,
        )

    safe = (rows - HOP // 2 - NFFT) // HOP + 1
    partners = (3, 1, 2)
    for k in range(chunks):
        for g in range(groups):
            first, last = 8 * g, min(8 * g + 8, used)
            if k == 0:
                loads[g].wait()
                lax.fori_loop(starts[g] // step, ends[g] // step, dequantize, 0)
                if g == 0:
                    pl.semaphore_wait(barrier, nt + nz - 1)
                    halo.start()
                if last > safe:
                    spectra(k, first, safe)
                    halo.wait()
                    first = safe
            spectra(k, first, last)
            for d in partners + (0,):
                pack_group(k, g, d)
                if d and k < chunks - 1:
                    exchange(k, g, d).start()
        if k == chunks - 1:
            for h in range(2):
                for d in partners:
                    exchange(k, h, d).start()

    width = nt * 2 * SLOTS
    wide = 2 * LANES
    eights = nt * groups
    lane_in = lax.broadcasted_iota(jnp.int32, (1, wide), 1) % 16 < 8
    sign = jnp.where(lane_in, -1.0, 1.0)

    def to_core(k, h):
        at = pl.ds(h * nz // 2, nz // 2)
        return pltpu.make_async_remote_copy(
            src_ref=part.at[k, at, 1 - c], dst_ref=corebuf.at[k, at],
            send_sem=core_s.at[k, h], recv_sem=core_r.at[k, h],
            device_id=(t, partner), device_id_type=MESH,
        )

    def to_z(k, peer):
        return pltpu.make_async_remote_copy(
            src_ref=summed.at[k, peer], dst_ref=zbuf.at[k, z],
            send_sem=z_s.at[k, peer], recv_sem=z_r.at[k, z],
            device_id=(t, peer * 2 + c), device_id_type=MESH,
        )

    def from_z(k, peer):
        return pltpu.make_async_remote_copy(
            src_ref=summed.at[k, peer], dst_ref=zbuf.at[k, peer],
            send_sem=z_s.at[k, peer], recv_sem=z_r.at[k, peer],
            device_id=(t, peer * 2 + c), device_id_type=MESH,
        )

    def to_tm(k, d):
        return pltpu.make_async_remote_copy(
            src_ref=gath.at[t, k], dst_ref=gath.at[t, k],
            send_sem=g_s.at[k, d - 1], recv_sem=g_r.at[k, d - 1],
            device_id=((t + d) % nt, p), device_id_type=MESH,
        )

    def cross_half(k, h):
        def cross(f, carry):
            stacked = recv[k, f].reshape(width, points)
            prod = lax.dot_general(
                stacked, stacked, (((1,), (1,)), ((), ())), preferred_element_type=jnp.float32
            )
            real = jnp.concatenate([prod[16 * m:16 * m + 8] for m in range(eights)], axis=0)
            imag = jnp.concatenate([prod[16 * m + 8:16 * m + 16] for m in range(eights)], axis=0)
            fill = jnp.zeros((nt * SLOTS, wide - width), jnp.float32)
            real = jnp.concatenate([real, fill], axis=1)
            imag = jnp.concatenate([imag, fill], axis=1)
            both = real + sign * imag
            both = both + pltpu.roll(both, wide - 8, 1)
            moved = pltpu.roll(both, wide - (LANES - 8), 1)
            part[k, f // 2, f % 2] = jnp.where(lane_in[:, :LANES], both[:, :LANES], moved[:, :LANES])
            return carry

        lax.fori_loop(h * half, (h + 1) * half, cross, 0)
        to_core(k, h).start()
        to_core(k, h).wait()
        for peer in range(h * nz // 2, (h + 1) * nz // 2):
            summed[k, peer] = part[k, peer, c] + corebuf[k, peer]

            @pl.when(peer != z)
            def _():
                to_z(k, peer).start()

    def compress(padded):
        kept = [padded[s * SLOTS:s * SLOTS + ranges[s][1]] for s in range(nt)]
        fill = LANES - sum(n for _, n in ranges)
        return jnp.concatenate(kept + [jnp.zeros((fill, LANES), jnp.float32)], axis=0)

    def reduce_z(k):
        total = summed[k, z]
        for d in range(1, nz):
            peer = (z + d) % nz
            from_z(k, peer).wait()
            total = total + zbuf[k, peer]
        full = jnp.concatenate([total, jnp.zeros((LANES - nt * SLOTS, LANES), jnp.float32)], axis=0)
        turned = full.T
        where = [16 * m if m < 8 else 16 * (m - 8) + 8 for m in range(eights)]
        turned = jnp.concatenate([turned[w:w + 8] for w in where], axis=0)
        gath[t, k] = compress(compress(turned).T)[:nt * SLOTS]
        for d in range(1, nt):
            to_tm(k, d).start()

    def finish(k):
        for d in range(1, nt):
            to_tm(k, d).wait()

        def one(s, carry):
            ordered = gath[s, k]
            fill = jnp.zeros((LANES - nt * SLOTS, LANES), jnp.float32)
            mirrored = jnp.concatenate([ordered, fill], axis=0).T[:nt * SLOTS]
            out_ref[s * chunks + k, 0] = 0.5 * (ordered + mirrored)
            out_ref[s * chunks + k, 1] = 0.5 * (ordered - mirrored)
            return carry

        lax.fori_loop(0, nt, one, 0)

    for k in range(chunks):
        for h in range(2):
            if k == chunks - 1:
                for d in partners:
                    exchange(k, h, d).wait()
            elif h == 0:
                for g in range(groups):
                    for d in partners:
                        exchange(k, g, d).wait()
            cross_half(k, h)
        if k < chunks - 1:
            reduce_z(k)
    for k in range(chunks - 1):
        finish(k)
    reduce_z(chunks - 1)
    finish(chunks - 1)


def fused(nt, np_, codes, scales, weights, freq_indices):
    rows, points = codes.shape
    nf = freq_indices.shape[0]
    nz = np_ // 2
    chunks = nf // (nt * np_)
    ranges = block_ranges(rows, nt)
    blocks = rows * nt // HOP - 1
    order = freq_indices.reshape(np_, nt, chunks).transpose(2, 1, 0).reshape(-1)
    cosine_table, sine_table = make_tables(order)
    shape = (chunks, nt * np_, NFFT)
    table = jnp.concatenate([cosine_table.reshape(shape), sine_table.reshape(shape)], axis=1)
    height = nt * SLOTS
    used = max(count for _, count in ranges)
    vals_rows = HOP // 2 + (used - 1) * HOP + NFFT
    groups = SLOTS // 8
    f32, bf16 = jnp.float32, jnp.bfloat16
    dma = pltpu.SemaphoreType.DMA
    vmem = pl.BlockSpec(memory_space=pltpu.VMEM)
    full = pl.pallas_call(
        functools.partial(kernel, nt, nz, chunks, ranges, points * np_),
        out_shape=jax.ShapeDtypeStruct((nt * chunks, 2, height, LANES), f32),
        in_specs=[pl.BlockSpec(memory_space=pl.ANY)] + [vmem] * 3,
        out_specs=vmem,
        scratch_shapes=[
            pltpu.VMEM((rows, points), bf16),
            pltpu.VMEM((vals_rows, points), bf16),
            pltpu.VMEM((points // LANES, nt * np_ * 2 * SLOTS, LANES), f32),
            pltpu.VMEM((chunks, nt - 1, np_, 2 * SLOTS, points), bf16),
            pltpu.VMEM((chunks, np_, nt, 2 * SLOTS, points), bf16),
            pltpu.VMEM((chunks, nz, 2, height, LANES), f32),
            pltpu.VMEM((chunks, nz, height, LANES), f32),
            pltpu.VMEM((chunks, nz, height, LANES), f32),
            pltpu.VMEM((chunks, nz, height, LANES), f32),
            pltpu.VMEM((nt, chunks, height, LANES), f32),
            dma((groups,)),
            dma, dma,
            dma((chunks, groups, nt - 1)), dma((chunks, groups, nt - 1)),
            dma((chunks, 2)), dma((chunks, 2)),
            dma((chunks, nz)), dma((chunks, nz)),
            dma((chunks, nt - 1)), dma((chunks, nt - 1)),
        ],
        compiler_params=pltpu.CompilerParams(
            collective_id=0, has_side_effects=True, vmem_limit_bytes=52 * 2**20
        ),
        name="spectra_cross",
    )(codes, scales.reshape(-1, 1), weights.reshape(1, -1), table)
    return full[:, :, :blocks, :blocks]


def cross_matrices(stacked):
    blocks = stacked.shape[1] // 2
    products = jnp.einsum("fip,fjp->fij", stacked, stacked, preferred_element_type=jnp.float32)
    matrix_re = products[:, :blocks, :blocks] + products[:, blocks:, blocks:]
    matrix_im = products[:, :blocks, blocks:] - products[:, blocks:, :blocks]
    return jnp.stack([matrix_re, matrix_im], axis=1)


def general(codes, scales, weights, freq_indices):
    values = (codes.astype(jnp.float32) * scales[:, None]).astype(jnp.bfloat16)
    regrouped = lax.all_to_all(values, "tm", split_axis=1, concat_axis=0, tiled=True)
    point_count = regrouped.shape[1]
    own_weights = lax.dynamic_slice_in_dim(
        weights, lax.axis_index("tm") * point_count, point_count, 0
    )
    total_points = weights.shape[0] * lax.axis_size("pts")
    root_weight = jnp.sqrt(own_weights / total_points)
    cosine_table, sine_table = make_tables(freq_indices)
    hop_rows = regrouped.reshape(-1, NFFT // 2, point_count)
    windows = jnp.concatenate([hop_rows[:-1], hop_rows[1:]], axis=1)
    real_part = jnp.einsum("fn,bnp->fbp", cosine_table, windows, preferred_element_type=jnp.float32)
    imag_part = jnp.einsum("fn,bnp->fbp", sine_table, windows, preferred_element_type=jnp.float32)
    scaled_re = (real_part * root_weight[None, None, :]).astype(jnp.bfloat16)
    scaled_im = (imag_part * root_weight[None, None, :]).astype(jnp.bfloat16)
    stacked = jnp.concatenate([scaled_re, scaled_im], axis=1)
    partial_value = lax.psum_scatter(
        cross_matrices(stacked), "pts", scatter_dimension=0, tiled=True
    )
    return lax.psum(partial_value, "tm")


def solution(mesh):
    nt, np_ = mesh.shape["tm"], mesh.shape["pts"]

    def per_device(codes, scales, weights, freq_indices):
        rows, points = codes.shape
        fits = (
            nt == 4
            and np_ == 8
            and freq_indices.shape[0] % (nt * np_) == 0
            and points % LANES == 0
            and rows % HALO == 0
            and rows % HOP == HOP // 2
            and max(count for _, count in block_ranges(rows, nt)) <= SLOTS
        )
        if fits:
            return fused(nt, np_, codes, scales, weights, freq_indices)
        return general(codes, scales, weights, freq_indices)

    return jax.shard_map(
        per_device,
        mesh=mesh,
        in_specs=(P("tm", "pts"), P("tm"), P("pts"), P()),
        out_specs=P("pts", None, None, None),
        check_vma=False,
    )
```

```python
import functools
import math

import jax
import jax.numpy as jnp
from jax import lax
from jax.experimental import pallas as pl
from jax.experimental.pallas import tpu as pltpu
from jax.sharding import PartitionSpec as P

NFFT = 256
HOP = NFFT // 2
HALO = 192
SLOTS = 24
LANES = 128
MESH = pl.DeviceIdType.MESH


def make_tables(freq_indices):
    sample = jnp.arange(NFFT, dtype=jnp.int32)
    phases = freq_indices[:, None] * sample[None, :] % NFFT
    angles = phases.astype(jnp.float32) * (2.0 * math.pi / NFFT)
    hann_window = 0.5 - 0.5 * jnp.cos(sample.astype(jnp.float32) * (2.0 * math.pi / NFFT))
    cosine_table = (0.25 * hann_window[None, :] * jnp.cos(angles)).astype(jnp.bfloat16)
    sine_table = (-0.25 * hann_window[None, :] * jnp.sin(angles)).astype(jnp.bfloat16)
    return (cosine_table, sine_table)


def block_ranges(rows, nt):
    blocks = rows * nt // HOP - 1
    firsts = [-(-t * rows // HOP) for t in range(nt)] + [blocks]
    return [(firsts[t], min(firsts[t + 1], blocks) - firsts[t]) for t in range(nt)]


def kernel(
    nt, nz, chunks, ranges, total_points,
    codes_hbm, scales_ref, weights_ref, table_ref, out_ref,
    codes_ref, vals, stage, send, recv, part, corebuf, summed, zbuf, gath,
    load_s, halo_s, halo_r, tm_s, tm_r, core_s, core_r, z_s, z_r, g_s, g_r,
):
    rows, points = codes_ref.shape
    t = lax.axis_index("tm")
    p = lax.axis_index("pts")
    z = p // 2
    c = p % 2
    partner = p + 1 - 2 * c
    per = 2 * nz
    half = per // 2
    lane_tiles = points // LANES
    groups = SLOTS // 8
    used = max(count for _, count in ranges)
    step = HALO // 2

    ends = [
        min(-(-(HOP // 2 + (8 * g + 7) * HOP + NFFT) // step) * step, rows) for g in range(groups - 1)
    ] + [rows]
    starts = [0] + ends[:-1]
    loads = [
        pltpu.make_async_copy(
            codes_hbm.at[pl.ds(starts[g], ends[g] - starts[g])],
            codes_ref.at[pl.ds(starts[g], ends[g] - starts[g])],
            load_s.at[g],
        )
        for g in range(groups)
    ]
    for load in loads:
        load.start()

    barrier = pltpu.get_barrier_semaphore()
    for d in range(1, nt):
        pl.semaphore_signal(barrier, inc=1, device_id=((t + d) % nt, p), device_id_type=MESH)
    pl.semaphore_signal(barrier, inc=1, device_id=(t, partner), device_id_type=MESH)
    for d in range(1, nz):
        pl.semaphore_signal(barrier, inc=1, device_id=(t, (z + d) % nz * 2 + c), device_id_type=MESH)

    root_weight = jnp.sqrt(weights_ref[...] / total_points).reshape(1, points)
    tail = vals.shape[0] - rows - HALO
    vals[pl.ds(rows + HALO, tail), :] = jnp.zeros((tail, points), jnp.bfloat16)
    half_rows = table_ref.shape[1] // 2

    def place(i, lane, result):
        at = (i // 8) * 16 + i % 8
        for part_of in range(2):
            stage[lane, pl.ds(at + 8 * part_of, half_rows, stride=2 * SLOTS), :] = result[part_of]

    for lane in range(lane_tiles):
        for spare in range(used, SLOTS):
            place(spare, lane, [jnp.zeros((half_rows, LANES), jnp.float32)] * 2)

    def dequantize(i, carry):
        at = pl.ds(pl.multiple_of(i * step, step), step)
        vals[at, :] = (codes_ref[at, :].astype(jnp.float32) * scales_ref[at, :]).astype(jnp.bfloat16)
        return carry

    halo = pltpu.make_async_remote_copy(
        src_ref=vals.at[pl.ds(0, HALO)],
        dst_ref=vals.at[pl.ds(rows, HALO)],
        send_sem=halo_s, recv_sem=halo_r,
        device_id=((t + nt - 1) % nt, p), device_id_type=MESH,
    )
    offset = (t % 2) * (HOP // 2)

    def spectra(k, first, last):
        table = table_ref[k]

        def spectrum(i, carry):
            window = vals[pl.ds(pl.multiple_of(offset + i * HOP, HOP // 2), NFFT), :]
            result = jnp.dot(table, window, preferred_element_type=jnp.float32) * root_weight
            for lane in range(lane_tiles):
                columns = result[:, lane * LANES:(lane + 1) * LANES]
                place(i, lane, [columns[:half_rows], columns[half_rows:]])
            return carry

        lax.fori_loop(first, last, spectrum, 0)

    def pack_group(k, g, d):
        dest = (t + d) % nt

        def pack(f, carry):
            base = pl.multiple_of((dest * per + f) * 2 * SLOTS + g * 16, 16)
            for lane in range(lane_tiles):
                block = stage[lane, pl.ds(base, 16), :].astype(jnp.bfloat16)
                at = slice(lane * LANES, (lane + 1) * LANES)
                if d == 0:
                    recv[k, f, t, g * 16:(g + 1) * 16, at] = block
                else:
                    send[k, d - 1, f, g * 16:(g + 1) * 16, at] = block
            return carry

        lax.fori_loop(0, per, pack, 0)

    def exchange(k, piece, d):
        if k < chunks - 1:
            src = send.at[k, d - 1, :, pl.ds(piece * 16, 16)]
            dst = recv.at[k, :, t, pl.ds(piece * 16, 16)]
        else:
            src = send.at[k, d - 1, pl.ds(piece * half, half)]
            dst = recv.at[k, pl.ds(piece * half, half), t]
        return pltpu.make_async_remote_copy(
            src_ref=src, dst_ref=dst,
            send_sem=tm_s.at[k, piece, d - 1], recv_sem=tm_r.at[k, piece, d - 1],
            device_id=((t + d) % nt, p), device_id_type=MESH,
        )

    safe = (rows - HOP // 2 - NFFT) // HOP + 1
    partners = (3, 1, 2)
    for k in range(chunks):
        for g in range(groups):
            first, last = 8 * g, min(8 * g + 8, used)
            if k == 0:
                loads[g].wait()
                lax.fori_loop(starts[g] // step, ends[g] // step, dequantize, 0)
                if g == 0:
                    pl.semaphore_wait(barrier, nt + nz - 1)
                    halo.start()
                if last > safe:
                    spectra(k, first, safe)
                    halo.wait()
                    first = safe
            spectra(k, first, last)
            for d in partners + (0,):
                pack_group(k, g, d)
                if d and k < chunks - 1:
                    exchange(k, g, d).start()
        if k == chunks - 1:
            for h in range(2):
                for d in partners:
                    exchange(k, h, d).start()

    width = nt * 2 * SLOTS
    wide = 2 * LANES
    eights = nt * groups
    lane_in = lax.broadcasted_iota(jnp.int32, (1, wide), 1) % 16 < 8
    sign = jnp.where(lane_in, -1.0, 1.0)

    def to_core(k, h):
        at = pl.ds(h * nz // 2, nz // 2)
        return pltpu.make_async_remote_copy(
            src_ref=part.at[k, at, 1 - c], dst_ref=corebuf.at[k, at],
            send_sem=core_s.at[k, h], recv_sem=core_r.at[k, h],
            device_id=(t, partner), device_id_type=MESH,
        )

    def to_z(k, peer):
        return pltpu.make_async_remote_copy(
            src_ref=summed.at[k, peer], dst_ref=zbuf.at[k, z],
            send_sem=z_s.at[k, peer], recv_sem=z_r.at[k, z],
            device_id=(t, peer * 2 + c), device_id_type=MESH,
        )

    def from_z(k, peer):
        return pltpu.make_async_remote_copy(
            src_ref=summed.at[k, peer], dst_ref=zbuf.at[k, peer],
            send_sem=z_s.at[k, peer], recv_sem=z_r.at[k, peer],
            device_id=(t, peer * 2 + c), device_id_type=MESH,
        )

    def to_tm(k, d):
        return pltpu.make_async_remote_copy(
            src_ref=gath.at[t, k], dst_ref=gath.at[t, k],
            send_sem=g_s.at[k, d - 1], recv_sem=g_r.at[k, d - 1],
            device_id=((t + d) % nt, p), device_id_type=MESH,
        )

    def cross_half(k, h):
        def cross(f, carry):
            stacked = recv[k, f].reshape(width, points)
            prod = lax.dot_general(
                stacked, stacked, (((1,), (1,)), ((), ())), preferred_element_type=jnp.float32
            )
            real = jnp.concatenate([prod[16 * m:16 * m + 8] for m in range(eights)], axis=0)
            imag = jnp.concatenate([prod[16 * m + 8:16 * m + 16] for m in range(eights)], axis=0)
            fill = jnp.zeros((nt * SLOTS, wide - width), jnp.float32)
            real = jnp.concatenate([real, fill], axis=1)
            imag = jnp.concatenate([imag, fill], axis=1)
            both = real + sign * imag
            both = both + pltpu.roll(both, wide - 8, 1)
            moved = pltpu.roll(both, wide - (LANES - 8), 1)
            part[k, f // 2, f % 2] = jnp.where(lane_in[:, :LANES], both[:, :LANES], moved[:, :LANES])
            return carry

        lax.fori_loop(h * half, (h + 1) * half, cross, 0)
        to_core(k, h).start()
        to_core(k, h).wait()
        for peer in range(h * nz // 2, (h + 1) * nz // 2):
            summed[k, peer] = part[k, peer, c] + corebuf[k, peer]

            @pl.when(peer != z)
            def _():
                to_z(k, peer).start()

    def compress(padded):
        kept = [padded[s * SLOTS:s * SLOTS + ranges[s][1]] for s in range(nt)]
        fill = LANES - sum(n for _, n in ranges)
        return jnp.concatenate(kept + [jnp.zeros((fill, LANES), jnp.float32)], axis=0)

    def reduce_z(k):
        total = summed[k, z]
        for d in range(1, nz):
            peer = (z + d) % nz
            from_z(k, peer).wait()
            total = total + zbuf[k, peer]
        full = jnp.concatenate([total, jnp.zeros((LANES - nt * SLOTS, LANES), jnp.float32)], axis=0)
        turned = full.T
        where = [16 * m if m < 8 else 16 * (m - 8) + 8 for m in range(eights)]
        turned = jnp.concatenate([turned[w:w + 8] for w in where], axis=0)
        gath[t, k] = compress(compress(turned).T)[:nt * SLOTS]
        for d in range(1, nt):
            to_tm(k, d).start()

    def finish(k):
        for d in range(1, nt):
            to_tm(k, d).wait()

        def one(s, carry):
            ordered = gath[s, k]
            fill = jnp.zeros((LANES - nt * SLOTS, LANES), jnp.float32)
            mirrored = jnp.concatenate([ordered, fill], axis=0).T[:nt * SLOTS]
            out_ref[s * chunks + k, 0] = 0.5 * (ordered + mirrored)
            out_ref[s * chunks + k, 1] = 0.5 * (ordered - mirrored)
            return carry

        lax.fori_loop(0, nt, one, 0)

    for k in range(chunks):
        for h in range(2):
            if k == chunks - 1:
                for d in partners:
                    exchange(k, h, d).wait()
            elif h == 0:
                for g in range(groups):
                    for d in partners:
                        exchange(k, g, d).wait()
            cross_half(k, h)
        if k < chunks - 1:
            reduce_z(k)
    for k in range(chunks - 1):
        finish(k)
    reduce_z(chunks - 1)
    finish(chunks - 1)


def fused(nt, np_, codes, scales, weights, freq_indices):
    rows, points = codes.shape
    nf = freq_indices.shape[0]
    nz = np_ // 2
    chunks = nf // (nt * np_)
    ranges = block_ranges(rows, nt)
    blocks = rows * nt // HOP - 1
    order = freq_indices.reshape(np_, nt, chunks).transpose(2, 1, 0).reshape(-1)
    cosine_table, sine_table = make_tables(order)
    shape = (chunks, nt * np_, NFFT)
    table = jnp.concatenate([cosine_table.reshape(shape), sine_table.reshape(shape)], axis=1)
    height = nt * SLOTS
    used = max(count for _, count in ranges)
    vals_rows = HOP // 2 + (used - 1) * HOP + NFFT
    groups = SLOTS // 8
    f32, bf16 = jnp.float32, jnp.bfloat16
    dma = pltpu.SemaphoreType.DMA
    vmem = pl.BlockSpec(memory_space=pltpu.VMEM)
    full = pl.pallas_call(
        functools.partial(kernel, nt, nz, chunks, ranges, points * np_),
        out_shape=jax.ShapeDtypeStruct((nt * chunks, 2, height, LANES), f32),
        in_specs=[pl.BlockSpec(memory_space=pl.ANY)] + [vmem] * 3,
        out_specs=vmem,
        scratch_shapes=[
            pltpu.VMEM((rows, points), bf16),
            pltpu.VMEM((vals_rows, points), bf16),
            pltpu.VMEM((points // LANES, nt * np_ * 2 * SLOTS, LANES), f32),
            pltpu.VMEM((chunks, nt - 1, np_, 2 * SLOTS, points), bf16),
            pltpu.VMEM((chunks, np_, nt, 2 * SLOTS, points), bf16),
            pltpu.VMEM((chunks, nz, 2, height, LANES), f32),
            pltpu.VMEM((chunks, nz, height, LANES), f32),
            pltpu.VMEM((chunks, nz, height, LANES), f32),
            pltpu.VMEM((chunks, nz, height, LANES), f32),
            pltpu.VMEM((nt, chunks, height, LANES), f32),
            dma((groups,)),
            dma, dma,
            dma((chunks, groups, nt - 1)), dma((chunks, groups, nt - 1)),
            dma((chunks, 2)), dma((chunks, 2)),
            dma((chunks, nz)), dma((chunks, nz)),
            dma((chunks, nt - 1)), dma((chunks, nt - 1)),
        ],
        compiler_params=pltpu.CompilerParams(
            collective_id=0, has_side_effects=True, vmem_limit_bytes=52 * 2**20
        ),
        name="spectra_cross",
    )(codes, scales.reshape(-1, 1), weights, table)
    return full[:, :, :blocks, :blocks]


def cross_matrices(stacked):
    blocks = stacked.shape[1] // 2
    products = jnp.einsum("fip,fjp->fij", stacked, stacked, preferred_element_type=jnp.float32)
    matrix_re = products[:, :blocks, :blocks] + products[:, blocks:, blocks:]
    matrix_im = products[:, :blocks, blocks:] - products[:, blocks:, :blocks]
    return jnp.stack([matrix_re, matrix_im], axis=1)


def general(codes, scales, weights, freq_indices):
    values = (codes.astype(jnp.float32) * scales[:, None]).astype(jnp.bfloat16)
    regrouped = lax.all_to_all(values, "tm", split_axis=1, concat_axis=0, tiled=True)
    point_count = regrouped.shape[1]
    own_weights = lax.dynamic_slice_in_dim(
        weights, lax.axis_index("tm") * point_count, point_count, 0
    )
    total_points = weights.shape[0] * lax.axis_size("pts")
    root_weight = jnp.sqrt(own_weights / total_points)
    cosine_table, sine_table = make_tables(freq_indices)
    hop_rows = regrouped.reshape(-1, NFFT // 2, point_count)
    windows = jnp.concatenate([hop_rows[:-1], hop_rows[1:]], axis=1)
    real_part = jnp.einsum("fn,bnp->fbp", cosine_table, windows, preferred_element_type=jnp.float32)
    imag_part = jnp.einsum("fn,bnp->fbp", sine_table, windows, preferred_element_type=jnp.float32)
    scaled_re = (real_part * root_weight[None, None, :]).astype(jnp.bfloat16)
    scaled_im = (imag_part * root_weight[None, None, :]).astype(jnp.bfloat16)
    stacked = jnp.concatenate([scaled_re, scaled_im], axis=1)
    partial_value = lax.psum_scatter(
        cross_matrices(stacked), "pts", scatter_dimension=0, tiled=True
    )
    return lax.psum(partial_value, "tm")


def solution(mesh):
    nt, np_ = mesh.shape["tm"], mesh.shape["pts"]

    def per_device(codes, scales, weights, freq_indices):
        rows, points = codes.shape
        fits = (
            nt == 4
            and np_ == 8
            and freq_indices.shape[0] % (nt * np_) == 0
            and points % LANES == 0
            and rows % HALO == 0
            and rows % HOP == HOP // 2
            and max(count for _, count in block_ranges(rows, nt)) <= SLOTS
        )
        if fits:
            return fused(nt, np_, codes, scales, weights, freq_indices)
        return general(codes, scales, weights, freq_indices)

    return jax.shard_map(
        per_device,
        mesh=mesh,
        in_specs=(P("tm", "pts"), P("tm"), P("pts"), P()),
        out_specs=P("pts", None, None, None),
        check_vma=False,
    )
```
